32 devices in a mesh: tiles: 8 (over z, y), samp: 4 (over x, core).
Axes of the slice: x: 2, y: 2, z: 4, core: 2. Of those that a mesh axis runs over, the one named last changes fastest.
Arguments:
- samples: bfloat16 [256, 8192], P('samp', 'tiles'), may hold values from -6 to 6
- omega: float32 [80, 512, 512], P('tiles', 'samp'), may hold values from -1 to 2, as said below
- coords: int32 [80, 2], P('tiles'), may hold values from 0 to 15, as said below
Outputs:
- updated: float32 [80, 512, 512], P('tiles', 'samp')
The draws below stay inside these ranges and needn't reach their ends.
Inputs may be any that keep to these rules, and one draw needn't show every extreme that they name: `coords`: tile k lies with index k // 10 of tiles. Write d for that index, and blocks d * 2 to (d + 1) * 2 - 1 as its own blocks; indices of devices wrap around. The first 2 tiles of d are the diagonal tiles (I, I) of its own blocks in order. Each other tile of d is (I, J) with I an own block and J a block of d + 1, or I a block of d - 1 and J a block of d + 1, or I < J both own blocks. No unordered pair of blocks appears twice in the whole list. `omega`: tiles with I == J are symmetric with diagonal entries from 0.5 to 2.
All inputs are finite; a program needn't handle non-finite values.
Results may differ from the reference program's by a relative error of at most 0.0023.
Values may be sent and summed in bfloat16 or wider, within the bound.
A program may use at most 64 MiB of HBM per device.

```python
import jax
import jax.numpy as jnp
from jax import lax

B = 512
BLK_DEV = 2
TILE_DEV = 10
ITERS = 2
NB = 16
P_SIZE = 8192
NS = 256
TILES = 80


def draw_coords(key, part):
    devices = NB // BLK_DEV

    def one_device(device, subkey):
        left_dev = (device - 1 + devices) % devices
        right_dev = (device + 1) % devices
        firsts = []
        seconds = []
        for first_pos in range(BLK_DEV):
            for second_pos in range(BLK_DEV):
                firsts.append(device * BLK_DEV + first_pos)
                seconds.append(right_dev * BLK_DEV + second_pos)
                firsts.append(left_dev * BLK_DEV + first_pos)
                seconds.append(right_dev * BLK_DEV + second_pos)
                if first_pos < second_pos:
                    firsts.append(device * BLK_DEV + first_pos)
                    seconds.append(device * BLK_DEV + second_pos)
        candidates = jnp.stack([jnp.stack(firsts), jnp.stack(seconds)], 1).astype(jnp.int32)
        order = jax.random.permutation(subkey, len(firsts))[:TILE_DEV - BLK_DEV]
        chosen = candidates[order]
        own_blocks = device * BLK_DEV + jnp.arange(BLK_DEV, dtype=jnp.int32)
        diagonal = jnp.stack([own_blocks, own_blocks], 1)
        return jnp.concatenate([diagonal, chosen], 0)
    subkeys = jax.random.split(jax.random.fold_in(key, 11), devices)
    result = jax.vmap(one_device)(jnp.arange(devices, dtype=jnp.int32), subkeys)
    return result.reshape(TILES, 2).astype(jnp.int32)


def draw_omega(key, part):
    key_off, key_diag = jax.random.split(jax.random.fold_in(key, 23), 2)
    raw = 0.03 * jax.random.normal(key_off, (TILES, B, B), jnp.float32)
    symmetric = (raw + jnp.swapaxes(raw, 1, 2)) * 0.7071
    slots = jnp.arange(TILES) % TILE_DEV
    is_diag = (slots < BLK_DEV)[:, None, None]
    tiles = jnp.where(is_diag, symmetric, raw)
    diag_vals = jnp.exp(jax.random.uniform(key_diag, (TILES, B), jnp.float32, jnp.log(0.5), jnp.log(2.0)))
    on_diagonal = jnp.eye(B, dtype=bool)[None]
    tiles = jnp.where(is_diag & on_diagonal, diag_vals[:, :, None], tiles)
    return tiles.astype(jnp.float32)


def levels(rng, extent, pieces, low, largest):
    def one(axis_at, blocks):
        steps = jax.random.uniform(jax.random.fold_in(jax.random.fold_in(rng, 6), axis_at), (blocks,), jnp.float32, low / len(pieces), largest / len(pieces))
        return jnp.repeat(jnp.exp(steps), extent[axis_at] // blocks).reshape((-1,) + (1,) * (len(extent) - axis_at - 1))

    gain = one(*pieces[0])
    for cut in pieces[1:]:
        gain = gain * one(*cut)
    return gain


def gaussian(own_key, dims, width, limit, pieces=(), held_as=jnp.bfloat16):
    values = width * jax.random.normal(own_key, dims, jnp.float32)
    if pieces:
        values = values * levels(own_key, dims, pieces, -0.22, 0.18)
    return jnp.clip(values, -limit, limit).astype(held_as)


def setup_inputs(seed: int = 0) -> dict:
    seeds = jax.random.split(jax.random.key(seed), 4)
    return {
        "samples": gaussian(seeds[0], (NS, P_SIZE), 1.0, 6.0, ((0, 4), (1, 8))),
        "omega": draw_omega(jax.random.fold_in(seeds[3], 71), 0),
        "coords": draw_coords(jax.random.fold_in(seeds[3], 71), 0),
    }


step_size = 0.25
penalty = 0.2

def take(matrix, start, count):
    return lax.dynamic_slice_in_dim(matrix, start, count, 1)

def put_add(totals, block, start):
    current = lax.dynamic_slice_in_dim(totals, start, block.shape[1], 1)
    return lax.dynamic_update_slice_in_dim(totals, current + block, start, 1)

def reference(samples, omega, coords):
    sample_full = samples.astype(jnp.float32)
    count = sample_full.shape[0]
    on_diagonal = jnp.eye(B, dtype=bool)
    for iteration in range(ITERS):
        omega_low = lax.optimization_barrier(omega.astype(jnp.bfloat16)).astype(jnp.float32)

        def contribute(totals, item):
            tile, pair = item
            row_start = pair[0] * B
            col_start = pair[1] * B
            off_diagonal = (pair[0] != pair[1]).astype(jnp.float32)
            to_col = jnp.dot(take(sample_full, row_start, B), tile, preferred_element_type=jnp.float32)
            to_row = jnp.dot(take(sample_full, col_start, B), tile.T, preferred_element_type=jnp.float32)
            totals = put_add(totals, to_col, col_start)
            totals = put_add(totals, to_row * off_diagonal, row_start)
            return (totals, None)
        products, unused = lax.scan(contribute, jnp.zeros(sample_full.shape, jnp.float32), (omega_low, coords))
        product_low = lax.optimization_barrier(products.astype(jnp.bfloat16)).astype(jnp.float32)

        def update(item):
            tile, pair = item
            row_start = pair[0] * B
            col_start = pair[1] * B
            first = jnp.dot(take(product_low, row_start, B).T, take(sample_full, col_start, B), preferred_element_type=jnp.float32)
            second = jnp.dot(take(sample_full, row_start, B).T, take(product_low, col_start, B), preferred_element_type=jnp.float32)
            grad = (first + second) / (2.0 * count)
            value = tile - step_size * grad
            shrunk = jnp.sign(value) * jnp.maximum(jnp.abs(value) - step_size * penalty, 0.0)
            positive = 0.5 * (value + jnp.sqrt(value * value + 4.0 * step_size))
            return jnp.where(on_diagonal & (pair[0] == pair[1]), positive, shrunk)
        omega = lax.map(update, (omega, coords))
    return omega
```

```python
import functools

import jax
import jax.numpy as jnp
from jax import lax
from jax.experimental import pallas as pl
from jax.experimental.pallas import tpu as pltpu
from jax.sharding import PartitionSpec as P

ITERS = 2
step_size = 0.25
penalty = 0.2

F32 = jnp.float32
BF16 = jnp.bfloat16
NN = (((1,), (0,)), ((), ()))
NT = (((1,), (1,)), ((), ()))
TN = (((0,), (0,)), ((), ()))


def dot(a, b, dims):
    return lax.dot_general(a, b, dims, preferred_element_type=F32)


def kernel(
    n, nt, nb, coords, x_ref, omega_hbm, out_hbm,
    om, xo, xr, xrow, ts, own_t, grads, sbf, sa, ra, sc, rc,
    to_left, from_right, to_right, from_left, prow, po, pr,
    load_sem, store_sem, send_sem, recv_sem,
):
    tiles, width = om.shape[0], om.shape[2]
    part = om.shape[1]
    rows = x_ref.shape[0]
    count = n * rows
    half = n // 2
    own_cols = nb * part
    d = lax.axis_index("tiles")
    q = lax.axis_index("samp")
    core = q % 2
    high = q // 2
    sib = q + 1 - 2 * core
    left = (d + nt - 1) % nt
    right = (d + 1) % nt
    at_sib = (d, sib)
    at_left = (left, q)
    at_right = (right, q)

    def at_high(r):
        return (d, (q + 2 * r) % n)

    load = pltpu.make_async_copy(omega_hbm, om, load_sem)
    load.start()

    barrier = pltpu.get_barrier_semaphore()
    peers = [at_sib, at_left, at_right] + [at_high(r) for r in range(1, half)]
    for peer in peers:
        pl.semaphore_signal(barrier, inc=1, device_id=peer, device_id_type=pl.DeviceIdType.MESH)
    pl.semaphore_wait(barrier, len(peers))

    sent = []

    def send(src, dst, device):
        slot = len(sent)
        copy = pltpu.make_async_remote_copy(
            src_ref=src, dst_ref=dst, send_sem=send_sem.at[slot], recv_sem=recv_sem.at[slot],
            device_id=device, device_id_type=pl.DeviceIdType.MESH,
        )
        copy.start()
        sent.append(copy)
        return copy

    def spread(src, buf):
        far = [send(src, buf.at[q], at_high(r)) for r in range(1, half)]
        near = [send(src, buf.at[q], at_sib)]
        return far, near

    def forward(buf, far, near):
        for r, copy in enumerate(far, 1):
            copy.wait_recv()
            origin = (q + n - 2 * r) % n
            near.append(send(buf.at[origin], buf.at[origin], at_sib))

    def arrived(near):
        for copy in near:
            copy.wait_recv()

    xr_in = send(x_ref, xr.at[q], at_left)
    far, near = spread(x_ref, xo)
    xo[q] = x_ref[...]

    blocks = nb * nt
    first = (d - 1) * nb
    stack = 2 * nb
    spots = []
    for k in range(tiles):
        i = coords[k, 0] - first
        i = jnp.where(i < 0, i + blocks, i)
        i = jnp.where(i >= blocks, i - blocks, i)
        j = coords[k, 1] - first
        j = jnp.where(j < 0, j + blocks, j)
        j = jnp.where(j >= blocks, j - blocks, j)
        spot = jnp.where(j >= stack, (j - stack) * stack + i, stack * nb + (i - nb) * nb + (j - nb))
        spots.append(jnp.clip(spot, 0, 3 * nb * nb - 1))

    def place(a, b):
        return stack * nb + a * nb + b

    def find(spot):
        slot = jnp.int32(0)
        held = jnp.int32(0)
        for k in range(nb, tiles):
            same = spots[k] == spot
            slot = jnp.where(same, k, slot)
            held = jnp.where(same, 1, held)
        return slot, held

    forward(xo, far, near)
    arrived(near)
    for b in range(nb):
        mine = xo[:, :, pl.ds(pl.multiple_of(b * width + q * part, part), part)]
        xrow[1, :, b * part:(b + 1) * part] = mine.reshape(count, part)
    xl_in = send(xrow.at[1], xrow.at[0], at_right)
    xr_in.wait_recv()
    far, near = spread(xr.at[q], xr)
    load.wait()

    def block_of(ref, b):
        return ref[:, :, b * width:(b + 1) * width].reshape(count, width)

    def gathered(ref, it, b):
        return jnp.concatenate([ref[it, s, :, b * part:(b + 1) * part] for s in range(n)], axis=1)

    where_right = [[find(j * stack + i) for i in range(stack)] for j in range(nb)]
    where_own = {(a, b): find(place(a, b)) for a in range(nb) for b in range(a + 1, nb)}

    for it in range(ITERS):
        for j in range(nb):
            for i in range(stack):
                slot, held = where_right[j][i]
                tile = jnp.where(held > 0, om[slot], 0.0)
                ts[j, i * part:(i + 1) * part, :] = tile.astype(BF16)
        for a in range(nb):
            own_t[a, a * part:(a + 1) * part, :] = om[a].astype(BF16)
        for (a, b), (slot, held) in where_own.items():
            tile = jnp.where(held > 0, om[slot], 0.0)
            own_t[b, a * part:(a + 1) * part, :] = tile.astype(BF16)
        if it == 0:
            xl_in.wait_recv()
        for j in range(nb):
            res = dot(xrow[0], ts[j, :own_cols, :], NN) + dot(xrow[1], ts[j, own_cols:, :], NN)
            for s in range(n):
                sbf[s, :, j * part:(j + 1) * part] = res[:, s * part:(s + 1) * part]
        for b in range(1, nb):
            res = dot(xrow[1, :, :b * part], own_t[b, :b * part, :], NN)
            at = (nb + b - 1) * part
            for s in range(n):
                sbf[s, :, at:at + part] = res[:, s * part:(s + 1) * part]
        pair = [None] * half
        for r in list(range(1, half)) + [0]:
            h = (high + r) % half
            sa[it, r] = sbf[2 * h + 1 - core].astype(BF16)
            pair[r] = send(sa.at[it, r], ra.at[it, r], at_sib)
        if it == 0:
            forward(xr, far, near)
            arrived(near)
        for b in range(nb):
            term = dot(block_of(xr, b), ts[b], NT)
            both = term if b == 0 else both + term
        to_left[it] = both[:, :own_cols].astype(BF16)
        in_right = send(to_left.at[it], from_right.at[it], at_left)
        cross = []
        for r in range(1, half):
            pair[r].wait_recv()
            h = (high + r) % half
            sc[it, r - 1] = (sbf[2 * h + core] + ra[it, r].astype(F32)).astype(BF16)
            cross.append(send(sc.at[it, r - 1], rc.at[it, r - 1], at_high(r)))
        own = [both[:, own_cols + a * part:own_cols + (a + 1) * part] for a in range(nb)]
        for b in range(nb):
            res = dot(block_of(xo, b), own_t[b, :(b + 1) * part, :], NT)
            for a in range(b + 1):
                own[a] = own[a] + res[:, a * part:(a + 1) * part]
        pair[0].wait_recv()
        total = sbf[q] + ra[it, 0].astype(F32)
        for r in range(1, half):
            cross[r - 1].wait_recv()
            total = total + rc[it, r - 1].astype(F32)
        to_right[it] = total[:, :own_cols].astype(BF16)
        in_left = send(to_right.at[it], from_left.at[it], at_right)
        for b in range(1, nb):
            at = (nb + b - 1) * part
            own[b] = own[b] + total[:, at:at + part]
        in_right.wait_recv()
        in_left.wait_recv()
        mine = jnp.concatenate(own, axis=1) + from_right[it].astype(F32) + from_left[it].astype(F32)
        prow[it, 1] = mine.astype(BF16)
        po[it, q] = mine.astype(BF16)

        pr_in = send(prow.at[it, 1], pr.at[it, q], at_left)
        pl_in = send(prow.at[it, 1], prow.at[it, 0], at_right)
        far, near = spread(prow.at[it, 1], po.at[it])
        pr_in.wait_recv()
        far_r, near_r = spread(pr.at[it, q], pr.at[it])
        forward(po.at[it], far, near)
        arrived(near)
        for b in range(nb):
            res = dot(prow[it, 1, :, :(b + 1) * part], block_of(xo, b), TN) + dot(
                xrow[1, :, :(b + 1) * part], gathered(po, it, b), TN
            )
            for a in range(b + 1):
                grads[place(a, b)] = res[a * part:(a + 1) * part, :]
        pl_in.wait_recv()
        forward(pr.at[it], far_r, near_r)
        arrived(near_r)
        for j in range(nb):
            right_p = gathered(pr, it, j)
            right_x = block_of(xr, j)
            for side in range(2):
                res = dot(prow[it, side], right_x, TN) + dot(xrow[side], right_p, TN)
                for a in range(nb):
                    grads[j * stack + side * nb + a] = res[a * part:(a + 1) * part, :]
        scale = step_size / (2.0 * count)
        edge = step_size * penalty
        row_ids = q * part + lax.broadcasted_iota(jnp.int32, (part, width), 0)
        col_ids = lax.broadcasted_iota(jnp.int32, (part, width), 1)
        for k in range(tiles):
            spot = place(k, k) if k < nb else spots[k]
            value = om[k] - scale * grads[spot]
            new = value - jnp.clip(value, -edge, edge)
            if k < nb:
                positive = 0.5 * (value + jnp.sqrt(value * value + 4.0 * step_size))
                new = jnp.where(row_ids == col_ids, positive, new)
            om[k] = new
            if it == ITERS - 1:
                pltpu.make_async_copy(om.at[k], out_hbm.at[k], store_sem.at[k]).start()

    for copy in sent:
        copy.wait_send()
    for k in range(tiles):
        pltpu.make_async_copy(om.at[k], out_hbm.at[k], store_sem.at[k]).wait()


def solution(mesh):
    n = mesh.shape["samp"]
    nt = mesh.shape["tiles"]

    def shards(samples, omega, coords):
        tiles, part, width = omega.shape
        rows, cols = samples.shape
        nb = cols // width
        count = n * rows
        half = n // 2
        own = nb * part
        extra = (2 * nb - 1) * part
        copies = (2 * n + 2) + ITERS * (half + half - 1 + 4 + 2 * (n - 1))
        vm = pltpu.VMEM
        scratch = [
            vm((tiles, part, width), F32),
            vm((n, rows, cols), BF16),
            vm((n, rows, cols), BF16),
            vm((2, count, own), BF16),
            vm((nb, 2 * own, width), BF16),
            vm((nb, own, width), BF16),
            vm((3 * nb * nb, part, width), F32),
            vm((n, count, extra), F32),
            vm((ITERS, half, count, extra), BF16),
            vm((ITERS, half, count, extra), BF16),
            vm((ITERS, half - 1, count, extra), BF16),
            vm((ITERS, half - 1, count, extra), BF16),
            vm((ITERS, count, own), BF16),
            vm((ITERS, count, own), BF16),
            vm((ITERS, count, own), BF16),
            vm((ITERS, count, own), BF16),
            vm((ITERS, 2, count, own), BF16),
            vm((ITERS, n, count, own), BF16),
            vm((ITERS, n, count, own), BF16),
            pltpu.SemaphoreType.DMA,
            pltpu.SemaphoreType.DMA((tiles,)),
            pltpu.SemaphoreType.DMA((copies,)),
            pltpu.SemaphoreType.DMA((copies,)),
        ]
        return pl.pallas_call(
            functools.partial(kernel, n, nt, nb),
            out_shape=jax.ShapeDtypeStruct(omega.shape, F32),
            in_specs=[
                pl.BlockSpec(memory_space=pltpu.SMEM),
                pl.BlockSpec(memory_space=pltpu.VMEM),
                pl.BlockSpec(memory_space=pl.ANY),
            ],
            out_specs=pl.BlockSpec(memory_space=pl.ANY),
            scratch_shapes=scratch,
            compiler_params=pltpu.CompilerParams(
                collective_id=0, has_side_effects=True, vmem_limit_bytes=48 * 1024 * 1024
            ),
        )(coords, samples, omega)

    in_specs = (P("samp", "tiles"), P("tiles", "samp", None), P("tiles", None))
    out_specs = P("tiles", "samp", None)
    return jax.shard_map(shards, mesh=mesh, in_specs=in_specs, out_specs=out_specs, check_vma=False)
```

```python
import functools

import jax
import jax.numpy as jnp
from jax import lax
from jax.experimental import pallas as pl
from jax.experimental.pallas import tpu as pltpu
from jax.sharding import PartitionSpec as P

ITERS = 2
step_size = 0.25
penalty = 0.2

F32 = jnp.float32
BF16 = jnp.bfloat16
NN = (((1,), (0,)), ((), ()))
NT = (((1,), (1,)), ((), ()))
TN = (((0,), (0,)), ((), ()))


def dot(a, b, dims):
    return lax.dot_general(a, b, dims, preferred_element_type=F32)


def kernel(
    n, nt, nb, coords, x_ref, omega_hbm, out_hbm,
    om, xo, xr, xrow, ts, own_t, grads, sbf, sa, ra, sc, rc,
    to_left, from_right, to_right, from_left, prow, po, pr,
    load_sem, store_sem, send_sem, recv_sem,
):
    tiles, width = om.shape[0], om.shape[2]
    part = om.shape[1]
    rows = x_ref.shape[0]
    count = n * rows
    half = n // 2
    own_cols = nb * part
    d = lax.axis_index("tiles")
    q = lax.axis_index("samp")
    core = q % 2
    high = q // 2
    sib = q + 1 - 2 * core
    left = (d + nt - 1) % nt
    right = (d + 1) % nt
    at_sib = (d, sib)
    at_left = (left, q)
    at_right = (right, q)

    def high_of(device, r):
        return (device, (q + 2 * r) % n)

    def origin(r):
        return (q + n - 2 * r) % n

    def at_high(r):
        return (d, (q + 2 * r) % n)

    load = pltpu.make_async_copy(omega_hbm, om, load_sem)
    load.start()

    barrier = pltpu.get_barrier_semaphore()
    peers = [at_sib] + [at_high(r) for r in range(1, half)]
    for r in range(n):
        peers += [(left, (q + r) % n), (right, (q + r) % n)]
    for peer in peers:
        pl.semaphore_signal(barrier, inc=1, device_id=peer, device_id_type=pl.DeviceIdType.MESH)
    pl.semaphore_wait(barrier, len(peers))

    sent = []

    def send(src, dst, device):
        slot = len(sent)
        copy = pltpu.make_async_remote_copy(
            src_ref=src, dst_ref=dst, send_sem=send_sem.at[slot], recv_sem=recv_sem.at[slot],
            device_id=device, device_id_type=pl.DeviceIdType.MESH,
        )
        copy.start()
        sent.append(copy)
        return copy

    def spread(src, buf):
        far = [send(src, buf.at[q], at_high(r)) for r in range(1, half)]
        near = [send(src, buf.at[q], at_sib)]
        return far, near

    def forward(buf, far, near):
        for r, copy in enumerate(far, 1):
            copy.wait_recv()
            near.append(send(buf.at[origin(r)], buf.at[origin(r)], at_sib))

    def arrived(near):
        for copy in near:
            copy.wait_recv()

    def spread_left(src, buf):
        return [(r, send(src, buf.at[q], high_of(left, r))) for r in list(range(1, half)) + [0]]

    def forward_all(buf, copies):
        near = []
        for r, copy in reversed(copies):
            copy.wait_recv()
            near.append(send(buf.at[origin(r)], buf.at[origin(r)], at_sib))
        return near

    own_rows = pl.ds(pl.multiple_of(q * rows, rows), rows)
    xl_in = []
    for r in range(n):
        other = (q + r) % n
        for b in range(nb):
            piece = pl.ds(pl.multiple_of(b * width + other * part, part), part)
            target = xrow.at[0, own_rows, pl.ds(b * part, part)]
            xl_in.append(send(x_ref.at[:, piece], target, (right, other)))
    far, near = spread(x_ref, xo)
    xr_in = spread_left(x_ref, xr)
    xo[q] = x_ref[...]

    blocks = nb * nt
    first = (d - 1) * nb
    stack = 2 * nb
    spots = []
    for k in range(tiles):
        i = coords[k, 0] - first
        i = jnp.where(i < 0, i + blocks, i)
        i = jnp.where(i >= blocks, i - blocks, i)
        j = coords[k, 1] - first
        j = jnp.where(j < 0, j + blocks, j)
        j = jnp.where(j >= blocks, j - blocks, j)
        spot = jnp.where(j >= stack, (j - stack) * stack + i, stack * nb + (i - nb) * nb + (j - nb))
        spots.append(jnp.clip(spot, 0, 3 * nb * nb - 1))

    def place(a, b):
        return stack * nb + a * nb + b

    def find(spot):
        slot = jnp.int32(0)
        held = jnp.int32(0)
        for k in range(nb, tiles):
            same = spots[k] == spot
            slot = jnp.where(same, k, slot)
            held = jnp.where(same, 1, held)
        return slot, held

    forward(xo, far, near)
    arrived(near)
    for b in range(nb):
        mine = xo[:, :, pl.ds(pl.multiple_of(b * width + q * part, part), part)]
        xrow[1, :, b * part:(b + 1) * part] = mine.reshape(count, part)
    load.wait()

    def block_of(ref, b):
        return ref[:, :, b * width:(b + 1) * width].reshape(count, width)

    def gathered(ref, it, b):
        return jnp.concatenate([ref[it, s, :, b * part:(b + 1) * part] for s in range(n)], axis=1)

    where_right = [[find(j * stack + i) for i in range(stack)] for j in range(nb)]
    where_own = {(a, b): find(place(a, b)) for a in range(nb) for b in range(a + 1, nb)}

    for it in range(ITERS):
        for j in range(nb):
            for i in range(stack):
                slot, held = where_right[j][i]
                tile = jnp.where(held > 0, om[slot], 0.0)
                ts[j, i * part:(i + 1) * part, :] = tile.astype(BF16)
        for a in range(nb):
            own_t[a, a * part:(a + 1) * part, :] = om[a].astype(BF16)
        for (a, b), (slot, held) in where_own.items():
            tile = jnp.where(held > 0, om[slot], 0.0)
            own_t[b, a * part:(a + 1) * part, :] = tile.astype(BF16)
        if it == 0:
            arrived(xl_in)
        for j in range(nb):
            res = dot(xrow[0], ts[j, :own_cols, :], NN) + dot(xrow[1], ts[j, own_cols:, :], NN)
            for s in range(n):
                sbf[s, :, j * part:(j + 1) * part] = res[:, s * part:(s + 1) * part]
        for b in range(1, nb):
            res = dot(xrow[1, :, :b * part], own_t[b, :b * part, :], NN)
            at = (nb + b - 1) * part
            for s in range(n):
                sbf[s, :, at:at + part] = res[:, s * part:(s + 1) * part]
        pair = [None] * half
        for r in list(range(1, half)) + [0]:
            h = (high + r) % half
            sa[it, r] = sbf[2 * h + 1 - core].astype(BF16)
            pair[r] = send(sa.at[it, r], ra.at[it, r], at_sib)
        cross = []
        in_left = []
        for r in list(range(1, half)) + [0]:
            pair[r].wait_recv()
            h = (high + r) % half
            total = sbf[2 * h + core] + ra[it, r].astype(F32)
            to_right[it, r] = total[:, :own_cols].astype(BF16)
            in_left.append(send(to_right.at[it, r], from_left.at[it, r], high_of(right, r)))
            if r > 0:
                sc[it, r - 1] = total[:, own_cols:].astype(BF16)
                cross.append(send(sc.at[it, r - 1], rc.at[it, r - 1], at_high(r)))
        total = total[:, own_cols:]
        if it == 0:
            arrived(forward_all(xr, xr_in))
        for b in range(nb):
            term = dot(block_of(xr, b), ts[b], NT)
            both = term if b == 0 else both + term
        to_left[it] = both[:, :own_cols].astype(BF16)
        in_right = send(to_left.at[it], from_right.at[it], at_left)
        own = [both[:, own_cols + a * part:own_cols + (a + 1) * part] for a in range(nb)]
        for b in range(nb):
            res = dot(block_of(xo, b), own_t[b, :(b + 1) * part, :], NT)
            for a in range(b + 1):
                own[a] = own[a] + res[:, a * part:(a + 1) * part]
        for r in range(1, half):
            cross[r - 1].wait_recv()
            total = total + rc[it, r - 1].astype(F32)
        for b in range(1, nb):
            own[b] = own[b] + total[:, (b - 1) * part:b * part]
        mine = jnp.concatenate(own, axis=1)
        arrived(in_left)
        for r in range(half):
            mine = mine + from_left[it, r].astype(F32)
        in_right.wait_recv()
        mine = mine + from_right[it].astype(F32)
        prow[it, 1] = mine.astype(BF16)

        pr_in = spread_left(prow.at[it, 1], pr.at[it])
        far, near = spread(prow.at[it, 1], po.at[it])
        pl_in = send(prow.at[it, 1], prow.at[it, 0], at_right)
        po[it, q] = prow[it, 1]
        forward(po.at[it], far, near)
        arrived(near)
        for b in range(nb):
            res = dot(prow[it, 1, :, :(b + 1) * part], block_of(xo, b), TN) + dot(
                xrow[1, :, :(b + 1) * part], gathered(po, it, b), TN
            )
            for a in range(b + 1):
                grads[place(a, b)] = res[a * part:(a + 1) * part, :]
        near = forward_all(pr.at[it], pr_in)
        arrived(near)
        for side in (1, 0):
            if side == 0:
                pl_in.wait_recv()
            for j in range(nb):
                res = dot(prow[it, side], block_of(xr, j), TN) + dot(xrow[side], gathered(pr, it, j), TN)
                for a in range(nb):
                    grads[j * stack + side * nb + a] = res[a * part:(a + 1) * part, :]
        scale = step_size / (2.0 * count)
        edge = step_size * penalty
        row_ids = q * part + lax.broadcasted_iota(jnp.int32, (part, width), 0)
        col_ids = lax.broadcasted_iota(jnp.int32, (part, width), 1)
        for k in range(tiles):
            spot = place(k, k) if k < nb else spots[k]
            value = om[k] - scale * grads[spot]
            new = value - jnp.clip(value, -edge, edge)
            if k < nb:
                positive = 0.5 * (value + jnp.sqrt(value * value + 4.0 * step_size))
                new = jnp.where(row_ids == col_ids, positive, new)
            om[k] = new
            if it == ITERS - 1:
                pltpu.make_async_copy(om.at[k], out_hbm.at[k], store_sem.at[k]).start()

    for copy in sent:
        copy.wait_send()
    for k in range(tiles):
        pltpu.make_async_copy(om.at[k], out_hbm.at[k], store_sem.at[k]).wait()


def solution(mesh):
    n = mesh.shape["samp"]
    nt = mesh.shape["tiles"]

    def shards(samples, omega, coords):
        tiles, part, width = omega.shape
        rows, cols = samples.shape
        nb = cols // width
        count = n * rows
        half = n // 2
        own = nb * part
        extra = (2 * nb - 1) * part
        copies = nb * n + 2 * n - 1 + ITERS * (3 * half + 1 + 2 * n - 1)
        vm = pltpu.VMEM
        scratch = [
            vm((tiles, part, width), F32),
            vm((n, rows, cols), BF16),
            vm((n, rows, cols), BF16),
            vm((2, count, own), BF16),
            vm((nb, 2 * own, width), BF16),
            vm((nb, own, width), BF16),
            vm((3 * nb * nb, part, width), F32),
            vm((n, count, extra), F32),
            vm((ITERS, half, count, extra), BF16),
            vm((ITERS, half, count, extra), BF16),
            vm((ITERS, half - 1, count, extra - own), BF16),
            vm((ITERS, half - 1, count, extra - own), BF16),
            vm((ITERS, count, own), BF16),
            vm((ITERS, count, own), BF16),
            vm((ITERS, half, count, own), BF16),
            vm((ITERS, half, count, own), BF16),
            vm((ITERS, 2, count, own), BF16),
            vm((ITERS, n, count, own), BF16),
            vm((ITERS, n, count, own), BF16),
            pltpu.SemaphoreType.DMA,
            pltpu.SemaphoreType.DMA((tiles,)),
            pltpu.SemaphoreType.DMA((copies,)),
            pltpu.SemaphoreType.DMA((copies,)),
        ]
        return pl.pallas_call(
            functools.partial(kernel, n, nt, nb),
            out_shape=jax.ShapeDtypeStruct(omega.shape, F32),
            in_specs=[
                pl.BlockSpec(memory_space=pltpu.SMEM),
                pl.BlockSpec(memory_space=pltpu.VMEM),
                pl.BlockSpec(memory_space=pltpu.HBM),
            ],
            out_specs=pl.BlockSpec(memory_space=pl.ANY),
            scratch_shapes=scratch,
            compiler_params=pltpu.CompilerParams(
                collective_id=0, has_side_effects=True, vmem_limit_bytes=48 * 1024 * 1024
            ),
        )(coords, samples, omega)

    in_specs = (P("samp", "tiles"), P("tiles", "samp", None), P("tiles", None))
    out_specs = P("tiles", "samp", None)
    return jax.shard_map(shards, mesh=mesh, in_specs=in_specs, out_specs=out_specs, check_vma=False)
```
